512 devices in a mesh: ctx: 32 (over y, z_hi, core), fsdp: 16 (over z_lo, x).
Axes of the slice: x: 4, y: 4, z: 16 (z_hi: 4, z_lo: 4; z = z_hi * 4 + z_lo), core: 2. Of those that a mesh axis runs over, the one named last changes fastest.
Arguments:
- events: bfloat16 [8192, 4096], P('ctx'), may hold values from -6 to 6
- tile_mask: int32 [64, 2], P('ctx'), may hold values 0 or 1
- initial_state: float32 [16, 128, 128], P('fsdp'), may hold values from -96 to 96
- w_query: bfloat16 [4096, 2048], P('ctx', 'fsdp'), may hold values from -0.09375 to 0.09375
- w_key: bfloat16 [4096, 2048], P('ctx', 'fsdp'), may hold values from -0.09375 to 0.09375
- w_value: bfloat16 [4096, 2048], P('ctx', 'fsdp'), may hold values from -0.09375 to 0.09375
- cotangent: bfloat16 [8192, 2048], P('ctx', 'fsdp'), may hold values from -6 to 6
Outputs:
- attended: bfloat16 [8192, 2048], P('ctx', 'fsdp')
- events_grad: bfloat16 [8192, 4096], P('ctx')
- query_grad: bfloat16 [4096, 2048], P('ctx', 'fsdp')
- key_grad: bfloat16 [4096, 2048], P('ctx', 'fsdp')
- value_grad: bfloat16 [4096, 2048], P('ctx', 'fsdp')
The draws below stay inside these ranges and needn't reach their ends.
Inputs may be any that keep to these rules, and one draw needn't show every extreme that they name: `tile_mask`: only entries whose column is not above the row's tile place within its block of 256 events are read.
All inputs are finite; a program needn't handle non-finite values.
Results may differ from the reference program's by a relative error of at most 0.03.
Values may be sent and summed in bfloat16 or wider, within the bound.
No kernel may reach another device: no remote copies, remote signals or barrier semaphores. Data moves between devices by JAX's collectives and lax.ppermute only.
A program may use at most 64 MiB of HBM per device.

```python
import jax
import jax.numpy as jnp
from jax import lax

D = 4096
HDIM = 128
HEAD_DEV = 1
HEADS = 16
TILE = 128
TOK_DEV = 256
TOKENS = 8192


def touch_ends(array, own_key, smallest, largest):
    longest = array.shape.index(max(array.shape))
    spots = []
    for shift in (0, 1):
        where = [jax.random.randint(jax.random.fold_in(own_key, axis), (), 0, length) for axis, length in enumerate(array.shape)]
        where[longest] = (where[longest] + shift) % array.shape[longest]
        spots.append(tuple(where))
    return array.at[spots[0]].set(smallest).at[spots[1]].set(largest)


def block_levels(own_key, extent, pieces, least, high):
    loudness, own = 1.0, jax.random.fold_in(own_key, 6)
    for axis_at, parts in pieces:
        heights = jnp.exp(jax.random.uniform(jax.random.fold_in(own, axis_at), (parts,), jnp.float32, least / len(pieces), high / len(pieces)))
        loudness = loudness * jnp.repeat(heights, extent[axis_at] // parts).reshape([-1 if axis == axis_at else 1 for axis in range(len(extent))])
    return loudness


def gaussian(own_key, dims, spread, reach, split=(), kind=jnp.bfloat16):
    factor_of = block_levels(own_key, dims, split, -0.22, 0.18) if split else 1.0
    array = jax.random.normal(own_key, dims, jnp.float32) * spread * factor_of
    return jnp.minimum(jnp.maximum(array, -reach), reach).astype(kind)


def setup_inputs(seed: int = 0) -> dict:
    keys = jax.random.split(jax.random.key(seed), 8)
    events = gaussian(keys[0], (TOKENS, D), 1.0, 6.0, ((0, 32),))
    tile_mask = touch_ends((jax.random.randint(keys[1], (TOKENS // TILE, TOK_DEV // TILE), 0, 4) < 3).astype(jnp.int32), jax.random.fold_in(keys[1], 1), 0, 1)
    initial_state = gaussian(keys[2], (HEADS, HDIM, HDIM), 16.0, 96.0, ((0, 16),), jnp.float32)
    w_query = gaussian(keys[3], (D, HEADS * HDIM), D ** -0.5, 0.09375, ((0, 32), (1, 16)))
    w_key = gaussian(keys[4], (D, HEADS * HDIM), D ** -0.5, 0.09375, ((0, 32), (1, 16)))
    w_value = gaussian(keys[5], (D, HEADS * HDIM), D ** -0.5, 0.09375, ((0, 32), (1, 16)))
    cotangent = gaussian(keys[6], (TOKENS, HEADS * HDIM), 1.0, 6.0, ((0, 32), (1, 16)))
    return dict(events=events, tile_mask=tile_mask, initial_state=initial_state, w_query=w_query, w_key=w_key, w_value=w_value, cotangent=cotangent)


epsilon = 1e-06

def allowed_pairs(mask_block, tile):
    count = mask_block.shape[0]
    size = count * tile
    row_index = lax.broadcasted_iota(jnp.int32, (size, size), 0)
    col_index = lax.broadcasted_iota(jnp.int32, (size, size), 1)
    tiled = jnp.repeat(jnp.repeat(mask_block, tile, axis=0), tile, axis=1)
    return jnp.where((col_index <= row_index) & (tiled > 0), 1.0, 0.0).astype(jnp.float32)

def block_forward(queries, key_rows, value_rows, carried_bf, allowed):
    scores = jnp.einsum('thd,shd->hts', queries.astype(jnp.float32), key_rows.astype(jnp.float32)) * allowed[None]
    mixing = scores.astype(jnp.bfloat16)
    mixture = jnp.einsum('hts,shd->thd', mixing.astype(jnp.float32), value_rows.astype(jnp.float32))
    mixture = mixture + jnp.einsum('thd,hde->the', queries.astype(jnp.float32), carried_bf.astype(jnp.float32))
    return (mixing, mixture)

def block_backward(queries, key_rows, value_rows, mixing, mixture_grad, carried_bf, later_bf, allowed):
    score_grad = (jnp.einsum('the,she->hts', mixture_grad.astype(jnp.float32), value_rows.astype(jnp.float32)) * allowed[None]).astype(jnp.bfloat16)
    sgrad = score_grad.astype(jnp.float32)
    query_part = jnp.einsum('hts,shd->thd', sgrad, key_rows.astype(jnp.float32))
    query_part = query_part + jnp.einsum('the,hde->thd', mixture_grad.astype(jnp.float32), carried_bf.astype(jnp.float32))
    key_part = jnp.einsum('hts,thd->shd', sgrad, queries.astype(jnp.float32))
    key_part = key_part + jnp.einsum('she,hde->shd', value_rows.astype(jnp.float32), later_bf.astype(jnp.float32))
    value_part = jnp.einsum('hts,the->she', mixing.astype(jnp.float32), mixture_grad.astype(jnp.float32))
    value_part = value_part + jnp.einsum('shd,hde->she', key_rows.astype(jnp.float32), later_bf.astype(jnp.float32))
    return (query_part.astype(jnp.bfloat16), key_part.astype(jnp.bfloat16), value_part.astype(jnp.bfloat16))

def reference(events, tile_mask, initial_state, w_query, w_key, w_value, cotangent):
    blocks = TOKENS // TOK_DEV
    count = TOK_DEV // TILE
    head_width = HEAD_DEV * HDIM
    groups = HEADS // HEAD_DEV
    masks = tile_mask.reshape(blocks, count, count)
    allowed = jax.vmap(lambda single: allowed_pairs(single, TILE))(masks)
    stacked = jnp.stack((w_query, w_key, w_value))
    event_blocks = events.reshape(blocks, TOK_DEV, D)

    def one_group(carry, index):
        start = (index * head_width).astype(jnp.int32)
        head_start = (index * HEAD_DEV).astype(jnp.int32)
        panels = lax.dynamic_slice_in_dim(stacked, start, head_width, 2)
        upstream_all = lax.dynamic_slice_in_dim(cotangent, start, head_width, 1)
        entering = lax.dynamic_slice_in_dim(initial_state, head_start, HEAD_DEV, 0)
        projected = [jnp.dot(events, panels[which], preferred_element_type=jnp.float32).astype(jnp.bfloat16) for which in range(3)]
        queries, key_rows, value_rows = [item.reshape(blocks, TOK_DEV, HEAD_DEV, HDIM) for item in projected]
        local_state = jnp.einsum('cthd,cthe->chde', key_rows.astype(jnp.float32), value_rows.astype(jnp.float32))
        running = jnp.cumsum(local_state, axis=0)
        zeros_state = jnp.zeros((1, HEAD_DEV, HDIM, HDIM), jnp.float32)
        carried = jnp.concatenate([zeros_state, running[:-1]], axis=0) + entering[None]
        carried_bf = carried.astype(jnp.bfloat16)
        mixing, mixture = jax.vmap(block_forward)(queries, key_rows, value_rows, carried_bf, allowed)
        inverse_rms = lax.rsqrt(lax.optimization_barrier(jnp.mean(mixture * mixture, axis=-1, keepdims=True)) + epsilon)
        attended = (mixture * inverse_rms).astype(jnp.bfloat16)
        upstream = upstream_all.reshape(blocks, TOK_DEV, HEAD_DEV, HDIM).astype(jnp.float32)
        mixture_grad = (inverse_rms * upstream - mixture * inverse_rms ** 3 * lax.optimization_barrier(jnp.mean(upstream * mixture, axis=-1, keepdims=True))).astype(jnp.bfloat16)
        local_grad = jnp.einsum('cthd,cthe->chde', queries.astype(jnp.float32), mixture_grad.astype(jnp.float32))
        backward_run = jnp.cumsum(local_grad[::-1], axis=0)[::-1]
        later = jnp.concatenate([backward_run[1:], zeros_state], axis=0)
        later_bf = later.astype(jnp.bfloat16)
        query_part, key_part, value_part = jax.vmap(block_backward)(queries, key_rows, value_rows, mixing, mixture_grad, carried_bf, later_bf, allowed)
        grads = jnp.stack([item.reshape(TOKENS, head_width) for item in (query_part, key_part, value_part)])
        term = jnp.einsum('ktw,kdw->td', grads.astype(jnp.float32), panels.astype(jnp.float32)).astype(jnp.bfloat16)
        carry = carry + term.astype(jnp.float32)
        grad_blocks = jnp.transpose(grads.reshape(3, blocks, TOK_DEV, head_width), (1, 0, 2, 3))

        def block_weight(pair):
            block_events, block_grads = pair
            return jnp.einsum('td,ktw->dkw', block_events.astype(jnp.float32), block_grads.astype(jnp.float32)).astype(jnp.bfloat16)
        weight_terms = lax.map(block_weight, (event_blocks, grad_blocks))
        weight_sum = lax.optimization_barrier(jnp.sum(weight_terms.astype(jnp.float32), axis=0)).astype(jnp.bfloat16)
        return (carry, (attended.reshape(TOKENS, head_width), weight_sum))
    initial = jnp.zeros((TOKENS, D), jnp.float32)
    total, (attended_all, weight_all) = lax.scan(one_group, initial, jnp.arange(groups, dtype=jnp.int32))
    attended_out = jnp.moveaxis(attended_all, 0, 1).reshape(TOKENS, HEADS * HDIM)
    outputs = []
    for which in range(3):
        outputs.append(jnp.moveaxis(weight_all[:, :, which, :], 0, 1).reshape(D, HEADS * HDIM))
    return (attended_out, total.astype(jnp.bfloat16), outputs[0], outputs[1], outputs[2])
```

```python
import jax
import jax.numpy as jnp
from jax import lax
from jax.sharding import Mesh
from jax.sharding import PartitionSpec as P

HDIM = 128
TILE = 128
CTX = ("y", "zh", "core")
FSDP = ("zl", "x")
SWAP = ((0, 1), (1, 0))
BF16, F32 = jnp.bfloat16, jnp.float32

epsilon = 1e-06


def dot(a, b, dims):
    return lax.dot_general(a, b, (dims, ((), ())), preferred_element_type=F32)


def mm(a, b):
    return dot(a, b, ((1,), (0,)))


def mt(a, b):
    return dot(a, b, ((1,), (1,)))


def tm(a, b):
    return dot(a, b, ((0,), (0,)))


def spread(array, axis):
    count = lax.axis_size(axis)
    return lax.all_to_all(jnp.broadcast_to(array[None], (count, *array.shape)), axis, 0, 0)


def trade(pieces, axis):
    return lax.all_to_all(pieces, axis, 0, 0)


def total(pieces):
    return jnp.sum(pieces.astype(F32), axis=0)


def swap(array):
    return lax.ppermute(array, "core", SWAP)


def allowed_pairs(mask_block):
    row_index = lax.broadcasted_iota(jnp.int32, (2 * TILE, 2 * TILE), 0)
    col_index = lax.broadcasted_iota(jnp.int32, (2 * TILE, 2 * TILE), 1)
    m = mask_block > 0
    lower = jnp.where(col_index < TILE, m[1, 0], m[1, 1])
    tiled = jnp.where(row_index < TILE, m[0, 0], lower)
    return (col_index <= row_index) & tiled


def scan_states(local, reverse, entering):
    blocks = 32
    rows = HDIM // blocks
    index = lax.axis_index(CTX)
    pieces = trade(local.astype(BF16).reshape(blocks, rows, HDIM), CTX)
    i = lax.broadcasted_iota(jnp.int32, (blocks, blocks), 0)
    j = lax.broadcasted_iota(jnp.int32, (blocks, blocks), 1)
    before = (j > i if reverse else j < i).astype(BF16)
    sums = mm(before, pieces.reshape(blocks, rows * HDIM)).reshape(blocks, rows, HDIM)
    if entering is not None:
        sums = sums + lax.dynamic_slice_in_dim(entering, index * rows, rows, 0)[None]
    return trade(sums.astype(BF16), CTX).reshape(HDIM, HDIM)


def gather_weights(shard):
    width = shard.shape[1]
    own = spread(spread(shard, "zh"), "y").reshape(2048, width)
    other = swap(own)
    back_own = trade(own.reshape(4, 512, width), "x")
    back_other = swap(back_own)
    return own, other, back_own, back_other


def scatter_grads(own, other):
    width = own.shape[1]
    mine = (own + swap(other.astype(BF16)).astype(F32)).astype(BF16)
    mine = total(trade(mine.reshape(4, 512, width), "y")).astype(BF16)
    return total(trade(mine.reshape(4, 128, width), "zh")).astype(BF16)


def on_device(events, tile_mask, initial_state, w_query, w_key, w_value, cotangent):
    first = lax.axis_index("core") == 0
    allowed = allowed_pairs(tile_mask)
    wkv, wkv_o, bkv, bkv_o = gather_weights(jnp.concatenate((w_key, w_value), axis=1))
    wq, wq_o, bq, bq_o = gather_weights(w_query)
    halves = events.reshape(256, 16, 2, 128)
    even, odd = halves[:, :, 0].reshape(256, 2048), halves[:, :, 1].reshape(256, 2048)
    ev, ev_o = jnp.where(first, even, odd), jnp.where(first, odd, even)

    kv = (mm(ev, wkv) + mm(ev_o, wkv_o)).astype(BF16)
    keys, values = kv[:, :128], kv[:, 128:]
    carried = scan_states(tm(keys, values), False, initial_state[0])
    queries = (mm(ev, wq) + mm(ev_o, wq_o)).astype(BF16)
    mixing = jnp.where(allowed, mt(queries, keys), 0.0).astype(BF16)
    mixture = mm(mixing, values) + mm(queries, carried)
    inverse_rms = lax.rsqrt(jnp.mean(mixture * mixture, axis=-1, keepdims=True) + epsilon)
    attended = (mixture * inverse_rms).astype(BF16)
    upstream = cotangent.astype(F32)
    mixture_grad = (
        inverse_rms * upstream
        - mixture * inverse_rms**3 * jnp.mean(upstream * mixture, axis=-1, keepdims=True)
    ).astype(BF16)
    later = scan_states(tm(queries, mixture_grad), True, None)
    score_grad = jnp.where(allowed, mt(mixture_grad, values), 0.0).astype(BF16)
    query_part = (mm(score_grad, keys) + mt(mixture_grad, carried)).astype(BF16)
    key_part = (tm(score_grad, queries) + mt(values, later)).astype(BF16)
    value_part = (tm(mixing, mixture_grad) + mm(keys, later)).astype(BF16)
    kv_part = jnp.concatenate((key_part, value_part), axis=1)

    def back(parts, own, other):
        seen = spread(parts, "x")
        a = sum(mt(seen[j], own[j]) for j in range(4))
        b = sum(mt(seen[j], other[j]) for j in range(4))
        return a, b

    qa, qb = back(query_part, bq, bq_o)
    ka, kb = back(kv_part, bkv, bkv_o)
    mine, others = (qa + ka).astype(BF16).reshape(256, 4, 1, 128), (qb + kb).astype(BF16).reshape(256, 4, 1, 128)
    term = jnp.where(
        first, jnp.concatenate((mine, others), 2), jnp.concatenate((others, mine), 2)
    ).reshape(256, 4, 256)
    summed = total(trade(term.transpose(1, 0, 2), "zl")).astype(BF16)
    whole = spread(spread(summed, "zl"), "x")
    events_grad = whole.transpose(2, 0, 1, 3).reshape(256, 4096)

    query_grad = scatter_grads(tm(ev, query_part), tm(ev_o, query_part))
    kv_grad = scatter_grads(tm(ev, kv_part), tm(ev_o, kv_part))
    return (attended, events_grad, query_grad, kv_grad[:, :128], kv_grad[:, 128:])


def solution(mesh):
    fine = Mesh(mesh.devices.reshape(4, 4, 2, 4, 4), CTX + FSDP)
    both = P(CTX, FSDP)
    return jax.shard_map(
        on_device,
        mesh=fine,
        in_specs=(P(CTX, None), P(CTX, None), P(FSDP, None, None), both, both, both, both),
        out_specs=(both, P(CTX, None), both, both, both),
        check_vma=False,
    )
```

```python
import jax
import jax.numpy as jnp
from jax import lax
from jax.experimental import pallas as pl
from jax.experimental.pallas import tpu as pltpu
from jax.sharding import Mesh
from jax.sharding import PartitionSpec as P

HDIM = 128
TILE = 128
CTX = ("y", "zh", "core")
FSDP = ("zl", "x")
SWAP = ((0, 1), (1, 0))
BF16, F32 = jnp.bfloat16, jnp.float32

epsilon = 1e-06


def dot(a, b, dims):
    return lax.dot_general(a, b, (dims, ((), ())), preferred_element_type=F32)


def mm(a, b):
    return dot(a, b, ((1,), (0,)))


def mt(a, b):
    return dot(a, b, ((1,), (1,)))


def tm(a, b):
    return dot(a, b, ((0,), (0,)))


def spread(array, axis):
    count = lax.axis_size(axis)
    return lax.all_to_all(jnp.broadcast_to(array[None], (count, *array.shape)), axis, 0, 0)


def trade(pieces, axis):
    return lax.all_to_all(pieces, axis, 0, 0)


def total(pieces):
    return jnp.sum(pieces.astype(F32), axis=0)


def swap(array):
    return lax.ppermute(array, "core", SWAP)


def allowed_pairs(mask_block):
    row_index = lax.broadcasted_iota(jnp.int32, (2 * TILE, 2 * TILE), 0)
    col_index = lax.broadcasted_iota(jnp.int32, (2 * TILE, 2 * TILE), 1)
    m = mask_block > 0
    lower = jnp.where(col_index < TILE, m[1, 0], m[1, 1])
    tiled = jnp.where(row_index < TILE, m[0, 0], lower)
    return (col_index <= row_index) & tiled


def scan_states(local, reverse, entering):
    chip, y = lax.axis_index(("zh", "core")), lax.axis_index("y")

    def reached(pieces, at):
        index = lax.broadcasted_iota(jnp.int32, (pieces.shape[0], 1, 1), 0)
        return jnp.sum(jnp.where(index > at if reverse else index < at, pieces, 0.0), axis=0)

    near = lax.all_gather(local.astype(BF16), ("zh", "core")).astype(F32)
    before = reached(near, chip)
    if entering is not None:
        before = before + entering
    lines = spread(jnp.sum(near, axis=0).astype(BF16), "y").astype(F32)
    return (before + reached(lines, y)).astype(BF16)


def params(steps_bytes, flops):
    return dict(
        compiler_params=pltpu.CompilerParams(vmem_limit_bytes=40 * 2**20),
        cost_estimate=pl.CostEstimate(flops=flops, bytes_accessed=steps_bytes, transcendentals=0),
    )


def half(core, which):
    return pl.ds(pl.multiple_of((core if which == 0 else 1 - core) * 128, 128), 128)


def project_kernel(ids, events, own, other, out, acc, both):
    step, core = pl.program_id(0), ids[0]

    @pl.when(step == 0)
    def _():
        acc[...] = jnp.zeros_like(acc)

    total = acc[...]
    for i in range(4):
        both[half(core, 0), :] = own[i]
        both[half(core, 1), :] = other[i]
        total = total + mm(events[:, i * 256 : (i + 1) * 256], both[...])
    acc[...] = total

    @pl.when(step == 3)
    def _():
        out[...] = acc[...].astype(BF16)


def project(ids, events, own, other):
    width = own.shape[-1]
    weights = pl.BlockSpec((4, 128, width), lambda g, _: (g, 0, 0))
    return pl.pallas_call(
        project_kernel,
        out_shape=jax.ShapeDtypeStruct((256, width), BF16),
        grid_spec=pltpu.PrefetchScalarGridSpec(
            num_scalar_prefetch=1,
            grid=(4,),
            in_specs=[pl.BlockSpec((256, 1024), lambda g, _: (0, g)), weights, weights],
            out_specs=pl.BlockSpec((256, width), lambda g, _: (0, 0)),
            scratch_shapes=[pltpu.VMEM((256, width), F32), pltpu.VMEM((256, width), BF16)],
        ),
        **params(5 * 2**20, 2 * 256 * 4096 * width),
    )(ids, events, own, other)


def pick_kernel(ids, own, after, *pieces):
    for k in range(4):
        pieces[k][...] = own[lax.rem(ids[1] + k, 4)]


def pick(ids, own, after):
    _, rows, width = own.shape
    whole = pl.BlockSpec(memory_space=pltpu.VMEM)
    return pl.pallas_call(
        pick_kernel,
        out_shape=[jax.ShapeDtypeStruct((rows, width), BF16)] * 4,
        in_specs=[pl.BlockSpec(memory_space=pltpu.SMEM), whole, pl.BlockSpec(memory_space=pl.ANY)],
        out_specs=[whole] * 4,
        **params(3 * 2**20, 0),
    )(ids, own, after)


def grads_kernel(ids, events, parts, after, own, other):
    for i in range(4):
        term = tm(events[:, i * 256 : (i + 1) * 256], parts[...]).astype(BF16)

        @pl.when(ids[0] == 0)
        def _():
            own[i], other[i] = term[:128], term[128:]

        @pl.when(ids[0] == 1)
        def _():
            own[i], other[i] = term[128:], term[:128]


def weight_terms(ids, events, parts, after):
    width = parts.shape[1]
    shape = jax.ShapeDtypeStruct((16, 128, width), BF16)
    terms = pl.BlockSpec((4, 128, width), lambda g, _: (g, 0, 0))
    return pl.pallas_call(
        grads_kernel,
        out_shape=(shape, shape),
        grid_spec=pltpu.PrefetchScalarGridSpec(
            num_scalar_prefetch=1,
            grid=(4,),
            in_specs=[
                pl.BlockSpec((256, 1024), lambda g, _: (0, g)),
                pl.BlockSpec((256, width), lambda g, _: (0, 0)),
                pl.BlockSpec(memory_space=pl.ANY),
            ],
            out_specs=(terms, terms),
        ),
        **params(5 * 2**20, 2 * 256 * 4096 * width),
    )(ids, events, parts, after)


def back_kernel(ids, seen, own, other, out, both):
    core, x = ids[0], ids[1]
    total = jnp.zeros((256, 256), F32)
    for k in range(4):
        both[k, half(core, 0), :] = own[k]
        both[k, half(core, 1), :] = other[k]
        total = total + mt(seen[lax.rem(x + 4 - k, 4)], both[k])
    out[...] = total.astype(BF16)


def back_terms(ids, seen, own, other):
    width = seen.shape[-1]
    weights = pl.BlockSpec((4, 128, width), lambda g, _: (0, g, 0))
    return pl.pallas_call(
        back_kernel,
        out_shape=jax.ShapeDtypeStruct((256, 1024), BF16),
        grid_spec=pltpu.PrefetchScalarGridSpec(
            num_scalar_prefetch=1,
            grid=(4,),
            in_specs=[pl.BlockSpec((4, 256, width), lambda g, _: (0, 0, 0)), weights, weights],
            out_specs=pl.BlockSpec((256, 256), lambda g, _: (0, g)),
            scratch_shapes=[pltpu.VMEM((4, 256, width), BF16)],
        ),
        **params(5 * 2**20, 2 * 256 * 4096 * width),
    )(ids, seen, own, other)


def lay_kernel(pieces, out):
    out[...] = pieces[0]


def lay_out(pieces):
    return pl.pallas_call(
        lay_kernel,
        out_shape=jax.ShapeDtypeStruct((256, 4096), BF16),
        grid=(4,),
        in_specs=[pl.BlockSpec((1, 256, 1024), lambda g: (g, 0, 0))],
        out_specs=pl.BlockSpec((256, 1024), lambda g: (0, g)),
        **params(4 * 2**20, 0),
    )(pieces)


def turn(axis, k):
    return [(i, (i + k) % 4) for i in range(4)]


def on_device(events, tile_mask, initial_state, w_query, w_key, w_value, cotangent):
    core, x = lax.axis_index("core"), lax.axis_index("x")
    ids = jnp.stack((core, x)).astype(jnp.int32)
    allowed = allowed_pairs(tile_mask)
    shard = jnp.concatenate((w_query, w_key, w_value), axis=1)
    own = spread(lax.all_gather(shard, "zh"), "y")
    other = swap(own)
    projected = project(ids, events, own.reshape(16, 128, 384), other.reshape(16, 128, 384))
    queries, keys, values = (projected[:, i * 128 : (i + 1) * 128] for i in range(3))
    carried = scan_states(tm(keys, values), False, initial_state[0])

    pieces = pick(ids, own.reshape(4, 512, 384), projected)
    pieces = [pieces[0]] + [lax.ppermute(pieces[k], "x", turn("x", k)) for k in (1, 2, 3)]
    back_own = jnp.stack(pieces)
    back_other = swap(back_own)

    mixing = jnp.where(allowed, mt(queries, keys), 0.0).astype(BF16)
    mixture = mm(mixing, values) + mm(queries, carried)
    inverse_rms = lax.rsqrt(jnp.mean(mixture * mixture, axis=-1, keepdims=True) + epsilon)
    attended = (mixture * inverse_rms).astype(BF16)
    upstream = cotangent.astype(F32)
    mixture_grad = (
        inverse_rms * upstream
        - mixture * inverse_rms**3 * jnp.mean(upstream * mixture, axis=-1, keepdims=True)
    ).astype(BF16)
    later = scan_states(tm(queries, mixture_grad), True, None)
    score_grad = jnp.where(allowed, mt(mixture_grad, values), 0.0).astype(BF16)
    query_part = (mm(score_grad, keys) + mt(mixture_grad, carried)).astype(BF16)
    key_part = (tm(score_grad, queries) + mt(values, later)).astype(BF16)
    value_part = (tm(mixing, mixture_grad) + mm(keys, later)).astype(BF16)
    parts = jnp.concatenate((query_part, key_part, value_part), axis=1)

    term = back_terms(ids, spread(parts, "x"), back_own, back_other)
    summed = total(trade(term.reshape(4, 64, 1024), "zl")).astype(BF16)
    events_grad = lay_out(spread(spread(summed, "zl").reshape(256, 1024), "x"))

    mine, others = weight_terms(ids, events, parts, swap(parts[:16, :128]))
    mine = (mine.astype(F32) + swap(others).astype(F32)).astype(BF16)
    mine = lax.psum_scatter(mine.reshape(2048, 384), "y", scatter_dimension=0, tiled=True)
    pieces = mine.reshape(4, 128, 384)
    zh = lax.axis_index("zh")
    pieces = [
        lax.dynamic_index_in_dim(pieces, lax.rem(zh + k, 4), 0, keepdims=False) for k in range(4)
    ]
    pieces = [pieces[0]] + [lax.ppermute(pieces[k], "zh", turn("zh", k)) for k in (1, 2, 3)]
    grads = sum(piece.astype(F32) for piece in pieces).astype(BF16)
    return (attended, events_grad, grads[:, :128], grads[:, 128:256], grads[:, 256:])


def solution(mesh):
    fine = Mesh(mesh.devices.reshape(4, 4, 2, 4, 4), CTX + FSDP)
    both = P(CTX, FSDP)
    return jax.shard_map(
        on_device,
        mesh=fine,
        in_specs=(P(CTX, None), P(CTX, None), P(FSDP, None, None), both, both, both, both),
        out_specs=(both, P(CTX, None), both, both, both),
        check_vma=False,
    )
```

```python
import jax
import jax.numpy as jnp
from jax import lax
from jax.experimental import pallas as pl
from jax.experimental.pallas import tpu as pltpu
from jax.sharding import Mesh
from jax.sharding import PartitionSpec as P

TILE = 128
CTX = ("y", "zh", "core")
FSDP = ("zl", "x")
BF16, F32 = jnp.bfloat16, jnp.float32
CORE, X, Y, ZH = range(4)

epsilon = 1e-06


def dot(a, b, dims):
    return lax.dot_general(a, b, (dims, ((), ())), preferred_element_type=F32)


def mm(a, b):
    return dot(a, b, ((1,), (0,)))


def mt(a, b):
    return dot(a, b, ((1,), (1,)))


def tm(a, b):
    return dot(a, b, ((0,), (0,)))


def shape(*dims, dtype=BF16):
    return jax.ShapeDtypeStruct(dims, dtype)


def spread(array, axis):
    count = lax.axis_size(axis)
    return lax.all_to_all(jnp.broadcast_to(array[None], (count, *array.shape)), axis, 0, 0)


def trade(pieces, axis):
    return lax.all_to_all(pieces, axis, 0, 0)


def swap(array):
    return lax.ppermute(array, "core", ((0, 1), (1, 0)))


def shift(piece, axis, k):
    return lax.ppermute(piece, axis, [(i, (i + k) % 4) for i in range(4)])


def turn(pieces, axis):
    return [pieces[0]] + [shift(pieces[k], axis, k) for k in (1, 2, 3)]


def params(data_bytes, flops=0, mib=24):
    return dict(
        compiler_params=pltpu.CompilerParams(vmem_limit_bytes=mib * 2**20),
        cost_estimate=pl.CostEstimate(flops=flops, bytes_accessed=data_bytes, transcendentals=0),
    )


VMEM = pl.BlockSpec(memory_space=pltpu.VMEM)
SMEM = pl.BlockSpec(memory_space=pltpu.SMEM)
ANY = pl.BlockSpec(memory_space=pl.ANY)


def half(core, base=0):
    return pl.ds(pl.multiple_of(base + core * 128, 128), 128)


def columns_kernel(ids, events, own, other, own_turned, other_turned):
    for i in range(4):
        place = slice(i * 128, (i + 1) * 128)
        for core, out, turned in ((0, own, own_turned), (1, other, other_turned)):
            core = ids[CORE] if core == 0 else 1 - ids[CORE]
            block = events[:, half(core, i * 256)]
            out[:, place] = block
            turned[place, :] = block.T


def columns(ids, events):
    wide = pl.BlockSpec((256, 512), lambda g, _: (0, g))
    tall = pl.BlockSpec((512, 256), lambda g, _: (g, 0))
    return pl.pallas_call(
        columns_kernel,
        out_shape=[shape(256, 2048)] * 2 + [shape(2048, 256)] * 2,
        grid_spec=pltpu.PrefetchScalarGridSpec(
            num_scalar_prefetch=1,
            grid=(4,),
            in_specs=[pl.BlockSpec((256, 1024), lambda g, _: (0, g))],
            out_specs=[wide, wide, tall, tall],
        ),
        **params(6 * 2**20),
    )(ids, events)


def project_kernel(own_events, other_events, own, other, rows, state):
    total = mm(own_events[...], own[...]) + mm(other_events[...], other[...])
    rows[...] = total.astype(BF16)
    state[...] = tm(rows[:, 128:256], rows[:, 256:]).astype(BF16)


def project(own_events, other_events, own, other):
    width = own.shape[-1]
    return pl.pallas_call(
        project_kernel,
        out_shape=(shape(256, width), shape(128, 128)),
        in_specs=[VMEM] * 4,
        out_specs=(VMEM, VMEM),
        **params(5 * 2**20, 2 * 256 * 4096 * width),
    )(own_events, other_events, own, other)


def pick(ids, own, after, shifts):
    def kernel(ids, own, after, *refs):
        pieces, sems = refs[:-1], refs[-1]
        moves = [
            pltpu.make_async_copy(own.at[lax.rem(ids[X] + k, 4)], piece, sems.at[i])
            for i, (k, piece) in enumerate(zip(shifts, pieces))
        ]
        for move in moves:
            move.start()
        for move in moves:
            move.wait()

    return pl.pallas_call(
        kernel,
        out_shape=[shape(*own.shape[1:])] * len(shifts),
        in_specs=[SMEM, ANY, ANY],
        out_specs=[ANY] * len(shifts),
        scratch_shapes=[pltpu.SemaphoreType.DMA((len(shifts),))],
        **params(3 * 2**20),
    )(ids, own, after)


def join_kernel(a, b, c, d, after, out, sems):
    moves = [
        pltpu.make_async_copy(piece, out.at[k], sems.at[k]) for k, piece in enumerate((a, b, c, d))
    ]
    for move in moves:
        move.start()
    for move in moves:
        move.wait()


def join(pieces, after):
    return pl.pallas_call(
        join_kernel,
        out_shape=shape(4, *pieces[0].shape),
        in_specs=[ANY] * 5,
        out_specs=ANY,
        scratch_shapes=[pltpu.SemaphoreType.DMA((4,))],
        **params(3 * 2**20),
    )(*pieces, after)


def prefix_kernel(reverse, ids, near, *refs):
    out, y = refs[-1], ids[Y]
    chip = ids[ZH] * 2 + ids[CORE]
    before = jnp.zeros((128, 128), F32) if reverse else refs[0][0]
    line = jnp.zeros((128, 128), F32)
    for i in range(8):
        term = near[i].astype(F32)
        line = line + term
        before = before + jnp.where(i > chip if reverse else i < chip, term, 0.0)
    for to in range(4):
        sent = jnp.where(y > to if reverse else y < to, line, 0.0)
        sent = jnp.where(y == to, before, sent).astype(BF16)
        if reverse:
            for x in range(4):
                out[to, x] = sent
        else:
            out[to] = sent


def prefix_terms(ids, near, entering=None):
    reverse = entering is None
    dims = (4, 4, 128, 128) if reverse else (4, 128, 128)
    return pl.pallas_call(
        lambda *refs: prefix_kernel(reverse, *refs),
        out_shape=shape(*dims),
        in_specs=[SMEM, VMEM] + [VMEM] * (not reverse),
        out_specs=VMEM,
        **params(2**20),
    )(ids, near, *(() if reverse else (entering,)))


def allowed_pairs(mask):
    row = lax.broadcasted_iota(jnp.int32, (2 * TILE, 2 * TILE), 0)
    col = lax.broadcasted_iota(jnp.int32, (2 * TILE, 2 * TILE), 1)
    lower = jnp.where(col < TILE, mask[1, 0], mask[1, 1])
    return (col <= row) & (jnp.where(row < TILE, mask[0, 0], lower) > 0)


def mix_kernel(mask, rows, mixing, within):
    queries, keys, values = (rows[:, i * 128 : (i + 1) * 128] for i in range(3))
    mixed = jnp.where(allowed_pairs(mask), mt(queries, keys), 0.0).astype(BF16)
    mixing[...] = mixed
    within[...] = mm(mixed, values)


def mix(mask, rows):
    return pl.pallas_call(
        mix_kernel,
        out_shape=(shape(256, 256), shape(256, 128, dtype=F32)),
        in_specs=[SMEM, VMEM],
        out_specs=(VMEM, VMEM),
        **params(2**20, 2 * 256 * 256 * 256),
    )(mask, rows)


def middle_kernel(mask, rows, mixing, within, states, cotangent, attended, early, local_grad):
    queries, keys, values = (rows[:, i * 128 : (i + 1) * 128] for i in range(3))
    carried = jnp.sum(states[...].astype(F32), axis=0).astype(BF16)
    mixture = within[...] + mm(queries, carried)
    inverse_rms = lax.rsqrt(jnp.mean(mixture * mixture, axis=-1, keepdims=True) + epsilon)
    attended[...] = (mixture * inverse_rms).astype(BF16)
    upstream = cotangent[...].astype(F32)
    mixture_grad = (
        inverse_rms * upstream
        - mixture * inverse_rms**3 * jnp.mean(upstream * mixture, axis=-1, keepdims=True)
    ).astype(BF16)
    local_grad[...] = tm(queries, mixture_grad).astype(BF16)
    score_grad = jnp.where(allowed_pairs(mask), mt(mixture_grad, values), 0.0).astype(BF16)
    early[:, :128] = (mm(score_grad, keys) + mt(mixture_grad, carried)).astype(BF16)
    early[:, 128:256] = tm(score_grad, queries).astype(BF16)
    early[:, 256:384] = tm(mixing[...], mixture_grad).astype(BF16)
    early[:, 384:] = rows[:, 128:]


def middle(mask, rows, mixing, within, states, cotangent):
    return pl.pallas_call(
        middle_kernel,
        out_shape=(shape(256, 128), shape(256, 640), shape(128, 128)),
        in_specs=[SMEM] + [VMEM] * 5,
        out_specs=(VMEM,) * 3,
        **params(2**20, 2**28),
    )(mask, rows, mixing, within, states, cotangent)


def finish(early, later, out):
    keys, values = early[:, 384:512], early[:, 512:]
    out[:, :128] = early[:, :128]
    out[:, 128:256] = (early[:, 128:256].astype(F32) + mt(values, later)).astype(BF16)
    out[:, 256:] = (early[:, 256:384].astype(F32) + mm(keys, later)).astype(BF16)


def later_state(states, x):
    return sum(states[y, x].astype(F32) for y in range(4)).astype(BF16)


def parts_kernel(ids, early, states, after, out):
    finish(early, later_state(states, ids[X]), out)


def own_parts(ids, early, states, after):
    return pl.pallas_call(
        parts_kernel,
        out_shape=shape(256, 384),
        in_specs=[SMEM, VMEM, VMEM, ANY],
        out_specs=VMEM,
        **params(2**20, 2**25),
    )(ids, early, states, after)


def back_kernel(ids, early, states, own, other, after, out, *scratch):
    core, x = ids[CORE], ids[X]
    parts, heads, mine, others, sems = scratch
    moves = [pltpu.make_async_copy(early.at[j], heads.at[j], sems.at[j]) for j in range(4)]
    moves.append(pltpu.make_async_copy(own, mine, sems.at[4]))
    moves.append(pltpu.make_async_copy(other, others, sems.at[5]))
    for move in moves:
        move.start()
    for j in range(4):
        moves[j].wait()
        finish(heads.at[j], later_state(states, j), parts.at[j])
    for i, place, weights in ((4, core, mine), (5, 1 - core, others)):
        moves[i].wait()
        total = sum(mt(parts[lax.rem(x + 4 - k, 4)], weights[k]) for k in range(4)).astype(BF16)
        for i in range(4):
            out[:, half(place, i * 256)] = total[:, i * 128 : (i + 1) * 128]


def back_terms(ids, early, states, own, other, after):
    return pl.pallas_call(
        back_kernel,
        out_shape=shape(256, 1024),
        in_specs=[SMEM, ANY, VMEM, ANY, ANY, ANY],
        out_specs=VMEM,
        scratch_shapes=[
            pltpu.VMEM((4, 256, 384), BF16),
            pltpu.VMEM((4, 256, 640), BF16),
            pltpu.VMEM((4, 512, 384), BF16),
            pltpu.VMEM((4, 512, 384), BF16),
            pltpu.SemaphoreType.DMA((6,)),
        ],
        **params(5 * 2**20, 2 * 256 * 4096 * 384),
    )(ids, early, states, own, other, after)


def grads_kernel(events, crossed, parts, other, out):
    for k in range(4):
        rows = slice(k * 512, (k + 1) * 512)
        term = mm(events[rows, :], parts[...]) + mm(crossed[rows, :], other[...])
        out[rows, :] = term.astype(BF16)


def weight_terms(events, crossed, parts, other):
    width = parts.shape[1]
    return pl.pallas_call(
        grads_kernel,
        out_shape=shape(2048, width),
        in_specs=[VMEM] * 4,
        out_specs=VMEM,
        **params(5 * 2**20, 2 * 256 * 4096 * width),
    )(events, crossed, parts, other)


def regroup_kernel(ids, grads, *pieces):
    for k in range(4):
        rows = pl.ds(pl.multiple_of(lax.rem(ids[ZH] + k, 4) * 128, 128), 128)
        pieces[k][...] = grads[rows, :]


def regroup(ids, grads):
    return pl.pallas_call(
        regroup_kernel,
        out_shape=[shape(128, 384)] * 4,
        in_specs=[SMEM, VMEM],
        out_specs=[VMEM] * 4,
        **params(2 * 2**20),
    )(ids, grads)


def sum_kernel(pieces, *refs):
    out = refs[-1]
    summed = sum(pieces[k].astype(F32) for k in range(4)).astype(BF16)
    for k in range(4):
        out[k] = summed


def summed_for_all(pieces, *after):
    return pl.pallas_call(
        sum_kernel,
        out_shape=shape(*pieces.shape),
        in_specs=[VMEM] + [ANY] * len(after),
        out_specs=VMEM,
        **params(2**20),
    )(pieces, *after)


def lay_kernel(pieces, out):
    out[...] = pieces[0]


def lay_out(pieces):
    return pl.pallas_call(
        lay_kernel,
        out_shape=shape(256, 4096),
        grid=(4,),
        in_specs=[pl.BlockSpec((1, 256, 1024), lambda g: (g, 0, 0))],
        out_specs=pl.BlockSpec((256, 1024), lambda g: (0, g)),
        **params(4 * 2**20),
    )(pieces)


def on_device(events, tile_mask, initial_state, w_query, w_key, w_value, cotangent):
    ids = jnp.stack([lax.axis_index(axis) for axis in ("core", "x", "y", "zh")]).astype(jnp.int32)
    shard = jnp.concatenate((w_query, w_key, w_value), axis=1)
    own = spread(lax.all_gather(shard, "zh"), "y").reshape(2048, 384)
    own_events, other_events, own_turned, other_turned = columns(ids, events)
    rows, local_state = project(own_events, other_events, own, swap(own))

    near = lax.all_gather(local_state, ("zh", "core"))
    states = trade(prefix_terms(ids, near, initial_state), "y")
    mixing, within = mix(tile_mask, rows)
    quarters = own.reshape(4, 512, 384)
    back = turn(pick(ids, quarters, near, range(4)), "x")

    attended, early, local_grad = middle(tile_mask, rows, mixing, within, states, cotangent)
    heads = lax.all_gather(early, "x")
    near = lax.all_gather(local_grad, ("zh", "core"))
    sent = prefix_terms(ids, near).reshape(16, 128, 128)
    back_own = join(back, sent)
    back_other = swap(back_own)
    crossed = swap(other_turned)
    states = trade(sent, ("y", "x")).reshape(4, 4, 128, 128)
    parts = own_parts(ids, early, states, crossed)

    grads = weight_terms(own_turned, crossed, parts, swap(parts))
    term = back_terms(ids, heads, states, back_own, back_other, grads)
    summed = summed_for_all(trade(term.reshape(4, 64, 1024), "zl"))
    gathered = trade(summed, "zl").reshape(256, 1024)
    events_grad = lay_out(spread(gathered, "x"))
    grads = lax.psum_scatter(grads, "y", scatter_dimension=0, tiled=True)
    pieces = turn(regroup(ids, grads), "zh")
    grads = sum(piece.astype(F32) for piece in pieces).astype(BF16)
    return (attended, events_grad, grads[:, :128], grads[:, 128:256], grads[:, 256:])


def solution(mesh):
    fine = Mesh(mesh.devices.reshape(4, 4, 2, 4, 4), CTX + FSDP)
    both = P(CTX, FSDP)
    return jax.shard_map(
        on_device,
        mesh=fine,
        in_specs=(P(CTX, None), P(CTX, None), P(FSDP, None, None), both, both, both, both),
        out_specs=(both, P(CTX, None), both, both, both),
        check_vma=False,
    )
```

```python
import jax
import jax.numpy as jnp
from jax import lax
from jax.experimental import pallas as pl
from jax.experimental.pallas import tpu as pltpu
from jax.sharding import Mesh
from jax.sharding import PartitionSpec as P

TILE = 128
CTX = ("y", "zh", "core")
FSDP = ("zl", "x")
BF16, F32 = jnp.bfloat16, jnp.float32
CORE, X, Y, ZH = range(4)

epsilon = 1e-06


def dot(a, b, dims):
    return lax.dot_general(a, b, (dims, ((), ())), preferred_element_type=F32)


def mm(a, b):
    return dot(a, b, ((1,), (0,)))


def mt(a, b):
    return dot(a, b, ((1,), (1,)))


def tm(a, b):
    return dot(a, b, ((0,), (0,)))


def shape(*dims, dtype=BF16):
    return jax.ShapeDtypeStruct(dims, dtype)


def spread(array, axis):
    count = lax.axis_size(axis)
    return lax.all_to_all(jnp.broadcast_to(array[None], (count, *array.shape)), axis, 0, 0)


def trade(pieces, axis):
    return lax.all_to_all(pieces, axis, 0, 0)


def swap(array):
    return lax.ppermute(array, "core", ((0, 1), (1, 0)))


def shift(piece, axis, k):
    return lax.ppermute(piece, axis, [(i, (i + k) % 4) for i in range(4)])


def turn(pieces, axis):
    return [pieces[0]] + [shift(pieces[k], axis, k) for k in (1, 2, 3)]


def params(data_bytes, flops=0, mib=24):
    return dict(
        compiler_params=pltpu.CompilerParams(vmem_limit_bytes=mib * 2**20),
        cost_estimate=pl.CostEstimate(flops=flops, bytes_accessed=data_bytes, transcendentals=0),
    )


VMEM = pl.BlockSpec(memory_space=pltpu.VMEM)
SMEM = pl.BlockSpec(memory_space=pltpu.SMEM)
ANY = pl.BlockSpec(memory_space=pl.ANY)


def half(core, base=0):
    return pl.ds(pl.multiple_of(base + core * 128, 128), 128)


def columns_kernel(ids, events, own, other, own_turned, other_turned):
    for i in range(4):
        place = slice(i * 128, (i + 1) * 128)
        for core, out, turned in ((0, own, own_turned), (1, other, other_turned)):
            core = ids[CORE] if core == 0 else 1 - ids[CORE]
            block = events[:, half(core, i * 256)]
            out[:, place] = block
            turned[place, :] = block.T


def columns(ids, events):
    wide = pl.BlockSpec((256, 512), lambda g, _: (0, g))
    tall = pl.BlockSpec((512, 256), lambda g, _: (g, 0))
    return pl.pallas_call(
        columns_kernel,
        out_shape=[shape(256, 2048)] * 2 + [shape(2048, 256)] * 2,
        grid_spec=pltpu.PrefetchScalarGridSpec(
            num_scalar_prefetch=1,
            grid=(4,),
            in_specs=[pl.BlockSpec((256, 1024), lambda g, _: (0, g))],
            out_specs=[wide, wide, tall, tall],
        ),
        **params(6 * 2**20),
    )(ids, events)


def project_kernel(own_events, other_events, own, other, rows, state):
    total = mm(own_events[...], own[...]) + mm(other_events[...], other[...])
    rows[...] = total.astype(BF16)
    state[...] = tm(rows[:, 128:256], rows[:, 256:]).astype(BF16)


def project(own_events, other_events, own, other):
    width = own.shape[-1]
    return pl.pallas_call(
        project_kernel,
        out_shape=(shape(256, width), shape(128, 128)),
        in_specs=[VMEM] * 4,
        out_specs=(VMEM, VMEM),
        **params(5 * 2**20, 2 * 256 * 4096 * width),
    )(own_events, other_events, own, other)


def pick(ids, own, after, shifts):
    def kernel(ids, own, after, *refs):
        pieces, sems = refs[:-1], refs[-1]
        moves = [
            pltpu.make_async_copy(own.at[lax.rem(ids[X] + k, 4)], piece, sems.at[i])
            for i, (k, piece) in enumerate(zip(shifts, pieces))
        ]
        for move in moves:
            move.start()
        for move in moves:
            move.wait()

    return pl.pallas_call(
        kernel,
        out_shape=[shape(*own.shape[1:])] * len(shifts),
        in_specs=[SMEM, ANY, ANY],
        out_specs=[ANY] * len(shifts),
        scratch_shapes=[pltpu.SemaphoreType.DMA((len(shifts),))],
        **params(3 * 2**20),
    )(ids, own, after)


def join_kernel(a, b, c, d, after, out, sems):
    moves = [
        pltpu.make_async_copy(piece, out.at[k], sems.at[k]) for k, piece in enumerate((a, b, c, d))
    ]
    for move in moves:
        move.start()
    for move in moves:
        move.wait()


def join(pieces, after):
    return pl.pallas_call(
        join_kernel,
        out_shape=shape(4, *pieces[0].shape),
        in_specs=[ANY] * 5,
        out_specs=ANY,
        scratch_shapes=[pltpu.SemaphoreType.DMA((4,))],
        **params(3 * 2**20),
    )(*pieces, after)


def prefix_kernel(reverse, ids, near, *refs):
    out, y = refs[-1], ids[Y]
    chip = ids[ZH] * 2 + ids[CORE]
    before = jnp.zeros((128, 128), F32) if reverse else refs[0][0]
    line = jnp.zeros((128, 128), F32)
    for i in range(8):
        term = near[i].astype(F32)
        line = line + term
        before = before + jnp.where(i > chip if reverse else i < chip, term, 0.0)
    for to in range(4):
        sent = jnp.where(y > to if reverse else y < to, line, 0.0)
        sent = jnp.where(y == to, before, sent).astype(BF16)
        if reverse:
            for x in range(4):
                out[to, x] = sent
        else:
            out[to] = sent


def prefix_terms(ids, near, entering=None):
    reverse = entering is None
    dims = (4, 4, 128, 128) if reverse else (4, 128, 128)
    return pl.pallas_call(
        lambda *refs: prefix_kernel(reverse, *refs),
        out_shape=shape(*dims),
        in_specs=[SMEM, VMEM] + [VMEM] * (not reverse),
        out_specs=VMEM,
        **params(2**20),
    )(ids, near, *(() if reverse else (entering,)))


def allowed_pairs(mask):
    row = lax.broadcasted_iota(jnp.int32, (2 * TILE, 2 * TILE), 0)
    col = lax.broadcasted_iota(jnp.int32, (2 * TILE, 2 * TILE), 1)
    lower = jnp.where(col < TILE, mask[1, 0], mask[1, 1])
    return (col <= row) & (jnp.where(row < TILE, mask[0, 0], lower) > 0)


def mix_kernel(mask, rows, mixing, within):
    queries, keys, values = (rows[:, i * 128 : (i + 1) * 128] for i in range(3))
    mixed = jnp.where(allowed_pairs(mask), mt(queries, keys), 0.0).astype(BF16)
    mixing[...] = mixed
    within[...] = mm(mixed, values)


def mix(mask, rows):
    return pl.pallas_call(
        mix_kernel,
        out_shape=(shape(256, 256), shape(256, 128, dtype=F32)),
        in_specs=[SMEM, VMEM],
        out_specs=(VMEM, VMEM),
        **params(2**20, 2 * 256 * 256 * 256),
    )(mask, rows)


def middle_kernel(mask, rows, mixing, within, states, cotangent, attended, early, local_grad):
    queries, keys, values = (rows[:, i * 128 : (i + 1) * 128] for i in range(3))
    carried = jnp.sum(states[...].astype(F32), axis=0).astype(BF16)
    mixture = within[...] + mm(queries, carried)
    inverse_rms = lax.rsqrt(jnp.mean(mixture * mixture, axis=-1, keepdims=True) + epsilon)
    attended[...] = (mixture * inverse_rms).astype(BF16)
    upstream = cotangent[...].astype(F32)
    mixture_grad = (
        inverse_rms * upstream
        - mixture * inverse_rms**3 * jnp.mean(upstream * mixture, axis=-1, keepdims=True)
    ).astype(BF16)
    local_grad[...] = tm(queries, mixture_grad).astype(BF16)
    score_grad = jnp.where(allowed_pairs(mask), mt(mixture_grad, values), 0.0).astype(BF16)
    early[:, :128] = (mm(score_grad, keys) + mt(mixture_grad, carried)).astype(BF16)
    early[:, 128:256] = tm(score_grad, queries).astype(BF16)
    early[:, 256:384] = tm(mixing[...], mixture_grad).astype(BF16)
    early[:, 384:] = rows[:, 128:]


def middle(mask, rows, mixing, within, states, cotangent):
    return pl.pallas_call(
        middle_kernel,
        out_shape=(shape(256, 128), shape(256, 640), shape(128, 128)),
        in_specs=[SMEM] + [VMEM] * 5,
        out_specs=(VMEM,) * 3,
        **params(2**20, 2**28),
    )(mask, rows, mixing, within, states, cotangent)


def finish(early, later, out):
    keys, values = early[:, 384:512], early[:, 512:]
    out[:, :128] = early[:, :128]
    out[:, 128:256] = (early[:, 128:256].astype(F32) + mt(values, later)).astype(BF16)
    out[:, 256:] = (early[:, 256:384].astype(F32) + mm(keys, later)).astype(BF16)


def later_state(states, x):
    return sum(states[y, x].astype(F32) for y in range(4)).astype(BF16)


def parts_kernel(ids, early, states, after, out):
    finish(early, later_state(states, ids[X]), out)


def own_parts(ids, early, states, after):
    return pl.pallas_call(
        parts_kernel,
        out_shape=shape(256, 384),
        in_specs=[SMEM, VMEM, VMEM, ANY],
        out_specs=VMEM,
        **params(2**20, 2**25),
    )(ids, early, states, after)


def back_kernel(ids, early, states, own, other, after, out, *scratch):
    core, x = ids[CORE], ids[X]
    parts, heads, mine, others, sems = scratch
    moves = [pltpu.make_async_copy(early.at[j], heads.at[j], sems.at[j]) for j in range(4)]
    moves.append(pltpu.make_async_copy(own, mine, sems.at[4]))
    moves.append(pltpu.make_async_copy(other, others, sems.at[5]))
    for move in moves:
        move.start()
    for j in range(4):
        moves[j].wait()
        finish(heads.at[j], later_state(states, j), parts.at[j])
    for i, place, weights in ((4, core, mine), (5, 1 - core, others)):
        moves[i].wait()
        total = sum(mt(parts[lax.rem(x + 4 - k, 4)], weights[k]) for k in range(4)).astype(BF16)
        for i in range(4):
            out[:, half(place, i * 256)] = total[:, i * 128 : (i + 1) * 128]


def back_terms(ids, early, states, own, other, after):
    return pl.pallas_call(
        back_kernel,
        out_shape=shape(256, 1024),
        in_specs=[SMEM, ANY, VMEM, ANY, ANY, ANY],
        out_specs=VMEM,
        scratch_shapes=[
            pltpu.VMEM((4, 256, 384), BF16),
            pltpu.VMEM((4, 256, 640), BF16),
            pltpu.VMEM((4, 512, 384), BF16),
            pltpu.VMEM((4, 512, 384), BF16),
            pltpu.SemaphoreType.DMA((6,)),
        ],
        **params(5 * 2**20, 2 * 256 * 4096 * 384),
    )(ids, early, states, own, other, after)


def grads_kernel(events, crossed, parts, other, out):
    for k in range(4):
        rows = slice(k * 512, (k + 1) * 512)
        term = mm(events[rows, :], parts[...]) + mm(crossed[rows, :], other[...])
        out[rows, :] = term.astype(BF16)


def weight_terms(events, crossed, parts, other):
    width = parts.shape[1]
    return pl.pallas_call(
        grads_kernel,
        out_shape=shape(2048, width),
        in_specs=[VMEM] * 4,
        out_specs=VMEM,
        **params(5 * 2**20, 2 * 256 * 4096 * width),
    )(events, crossed, parts, other)


def regroup_kernel(ids, grads, *pieces):
    for k in range(4):
        rows = pl.ds(pl.multiple_of(lax.rem(ids[ZH] + k, 4) * 128, 128), 128)
        pieces[k][...] = grads[rows, :]


def regroup(ids, grads):
    return pl.pallas_call(
        regroup_kernel,
        out_shape=[shape(128, 384)] * 4,
        in_specs=[SMEM, VMEM],
        out_specs=[VMEM] * 4,
        **params(2 * 2**20),
    )(ids, grads)


def sum_kernel(pieces, *refs):
    out = refs[-1]
    summed = sum(pieces[k].astype(F32) for k in range(4)).astype(BF16)
    for k in range(4):
        out[k] = summed


def summed_for_all(pieces, *after):
    return pl.pallas_call(
        sum_kernel,
        out_shape=shape(*pieces.shape),
        in_specs=[VMEM] + [ANY] * len(after),
        out_specs=VMEM,
        **params(2**20),
    )(pieces, *after)


def lay_kernel(pieces, out):
    out[...] = pieces[0]


def lay_out(pieces):
    return pl.pallas_call(
        lay_kernel,
        out_shape=shape(256, 4096),
        grid=(4,),
        in_specs=[pl.BlockSpec((1, 256, 1024), lambda g: (g, 0, 0))],
        out_specs=pl.BlockSpec((256, 1024), lambda g: (0, g)),
        **params(4 * 2**20),
    )(pieces)


def on_device(events, tile_mask, initial_state, w_query, w_key, w_value, cotangent):
    ids = jnp.stack([lax.axis_index(axis) for axis in ("core", "x", "y", "zh")]).astype(jnp.int32)
    shard = jnp.concatenate((w_query, w_key, w_value), axis=1)
    own = spread(lax.all_gather(shard, "zh"), "y").reshape(2048, 384)
    own_events, other_events, own_turned, other_turned = columns(ids, events)
    rows, local_state = project(own_events, other_events, own, swap(own))

    near = lax.all_gather(local_state, ("zh", "core"))
    states = trade(prefix_terms(ids, near, initial_state), "y")
    mixing, within = mix(tile_mask, rows)
    quarters = own.reshape(4, 512, 384)
    back = turn(pick(ids, quarters, near, range(4)), "x")

    attended, early, local_grad = middle(tile_mask, rows, mixing, within, states, cotangent)
    heads = lax.all_gather(early, "x")
    near = lax.all_gather(local_grad, ("zh", "core"))
    sent = prefix_terms(ids, near).reshape(16, 128, 128)
    back_own = join(back, sent)
    back_other = swap(back_own)
    crossed = swap(other_turned)
    states = trade(sent, ("y", "x")).reshape(4, 4, 128, 128)
    parts = own_parts(ids, early, states, crossed)

    grads = weight_terms(own_turned, crossed, parts, swap(parts))
    term = back_terms(ids, heads, states, back_own, back_other, parts)
    summed = summed_for_all(trade(term.reshape(4, 64, 1024), "zl"))
    gathered = trade(summed, "zl").reshape(256, 1024)
    events_grad = lay_out(spread(gathered, "x"))
    grads = lax.psum_scatter(grads, "y", scatter_dimension=0, tiled=True)
    pieces = turn(regroup(ids, grads), "zh")
    grads = sum(piece.astype(F32) for piece in pieces).astype(BF16)
    return (attended, events_grad, grads[:, :128], grads[:, 128:256], grads[:, 256:])


def solution(mesh):
    fine = Mesh(mesh.devices.reshape(4, 4, 2, 4, 4), CTX + FSDP)
    both = P(CTX, FSDP)
    return jax.shard_map(
        on_device,
        mesh=fine,
        in_specs=(P(CTX, None), P(CTX, None), P(FSDP, None, None), both, both, both, both),
        out_specs=(both, P(CTX, None), both, both, both),
        check_vma=False,
    )
```

```python
import jax
import jax.numpy as jnp
from jax import lax
from jax.experimental import pallas as pl
from jax.experimental.pallas import tpu as pltpu
from jax.sharding import Mesh
from jax.sharding import PartitionSpec as P

TILE = 128
CTX = ("y", "zh", "core")
FSDP = ("zl", "x")
BF16, F32 = jnp.bfloat16, jnp.float32
CORE, X, Y, ZH = range(4)

epsilon = 1e-06


def dot(a, b, dims):
    return lax.dot_general(a, b, (dims, ((), ())), preferred_element_type=F32)


def mm(a, b):
    return dot(a, b, ((1,), (0,)))


def mt(a, b):
    return dot(a, b, ((1,), (1,)))


def tm(a, b):
    return dot(a, b, ((0,), (0,)))


def shape(*dims, dtype=BF16):
    return jax.ShapeDtypeStruct(dims, dtype)


def spread(array, axis):
    count = lax.axis_size(axis)
    return lax.all_to_all(jnp.broadcast_to(array[None], (count, *array.shape)), axis, 0, 0)


def trade(pieces, axis):
    return lax.all_to_all(pieces, axis, 0, 0)


def swap(array):
    return lax.ppermute(array, "core", ((0, 1), (1, 0)))


def shift(piece, axis, k):
    return lax.ppermute(piece, axis, [(i, (i + k) % 4) for i in range(4)])


def turn(pieces, axis):
    return [pieces[0]] + [shift(pieces[k], axis, k) for k in (1, 2, 3)]


def params(data_bytes, flops=0, mib=24):
    return dict(
        compiler_params=pltpu.CompilerParams(vmem_limit_bytes=mib * 2**20),
        cost_estimate=pl.CostEstimate(flops=flops, bytes_accessed=data_bytes, transcendentals=0),
    )


VMEM = pl.BlockSpec(memory_space=pltpu.VMEM)
SMEM = pl.BlockSpec(memory_space=pltpu.SMEM)
ANY = pl.BlockSpec(memory_space=pl.ANY)


def half(core, base=0):
    return pl.ds(pl.multiple_of(base + core * 128, 128), 128)


def columns_kernel(ids, events, own, other, own_turned, other_turned):
    for i in range(4):
        place = slice(i * 128, (i + 1) * 128)
        for core, out, turned in ((0, own, own_turned), (1, other, other_turned)):
            core = ids[CORE] if core == 0 else 1 - ids[CORE]
            block = events[:, half(core, i * 256)]
            out[:, place] = block
            turned[place, :] = block.T


def columns(ids, events):
    wide = pl.BlockSpec((256, 512), lambda g, _: (0, g))
    tall = pl.BlockSpec((512, 256), lambda g, _: (g, 0))
    return pl.pallas_call(
        columns_kernel,
        out_shape=[shape(256, 2048)] * 2 + [shape(2048, 256)] * 2,
        grid_spec=pltpu.PrefetchScalarGridSpec(
            num_scalar_prefetch=1,
            grid=(4,),
            in_specs=[pl.BlockSpec((256, 1024), lambda g, _: (0, g))],
            out_specs=[wide, wide, tall, tall],
        ),
        **params(6 * 2**20),
    )(ids, events)


def project_kernel(own_events, other_events, own, other, rows, state):
    total = mm(own_events[...], own[...]) + mm(other_events[...], other[...])
    rows[...] = total.astype(BF16)
    state[...] = tm(rows[:, 128:256], rows[:, 256:]).astype(BF16)


def project(own_events, other_events, own, other):
    width = own.shape[-1]
    return pl.pallas_call(
        project_kernel,
        out_shape=(shape(256, width), shape(128, 128)),
        in_specs=[VMEM] * 4,
        out_specs=(VMEM, VMEM),
        **params(5 * 2**20, 2 * 256 * 4096 * width),
    )(own_events, other_events, own, other)


def pick(ids, own, after, shifts):
    def kernel(ids, own, after, *refs):
        pieces, sems = refs[:-1], refs[-1]
        moves = [
            pltpu.make_async_copy(own.at[lax.rem(ids[X] + k, 4)], piece, sems.at[i])
            for i, (k, piece) in enumerate(zip(shifts, pieces))
        ]
        for move in moves:
            move.start()
        for move in moves:
            move.wait()

    return pl.pallas_call(
        kernel,
        out_shape=[shape(*own.shape[1:])] * len(shifts),
        in_specs=[SMEM, ANY, ANY],
        out_specs=[ANY] * len(shifts),
        scratch_shapes=[pltpu.SemaphoreType.DMA((len(shifts),))],
        **params(3 * 2**20),
    )(ids, own, after)


def join_kernel(a, b, c, d, after, out, sems):
    moves = [
        pltpu.make_async_copy(piece, out.at[k], sems.at[k]) for k, piece in enumerate((a, b, c, d))
    ]
    for move in moves:
        move.start()
    for move in moves:
        move.wait()


def join(pieces, after):
    return pl.pallas_call(
        join_kernel,
        out_shape=shape(4, *pieces[0].shape),
        in_specs=[ANY] * 5,
        out_specs=ANY,
        scratch_shapes=[pltpu.SemaphoreType.DMA((4,))],
        **params(3 * 2**20),
    )(*pieces, after)


def prefix_kernel(reverse, ids, near, *refs):
    out, y = refs[-1], ids[Y]
    chip = ids[ZH] * 2 + ids[CORE]
    before = jnp.zeros((128, 128), F32) if reverse else refs[0][0]
    line = jnp.zeros((128, 128), F32)
    for i in range(8):
        term = near[i].astype(F32)
        line = line + term
        before = before + jnp.where(i > chip if reverse else i < chip, term, 0.0)
    for to in range(4):
        sent = jnp.where(y > to if reverse else y < to, line, 0.0)
        sent = jnp.where(y == to, before, sent).astype(BF16)
        if reverse:
            for x in range(4):
                out[to, x] = sent
        else:
            out[to] = sent


def prefix_terms(ids, near, entering=None):
    reverse = entering is None
    dims = (4, 4, 128, 128) if reverse else (4, 128, 128)
    return pl.pallas_call(
        lambda *refs: prefix_kernel(reverse, *refs),
        out_shape=shape(*dims),
        in_specs=[SMEM, VMEM] + [VMEM] * (not reverse),
        out_specs=VMEM,
        **params(2**20),
    )(ids, near, *(() if reverse else (entering,)))


def allowed_pairs(mask):
    row = lax.broadcasted_iota(jnp.int32, (2 * TILE, 2 * TILE), 0)
    col = lax.broadcasted_iota(jnp.int32, (2 * TILE, 2 * TILE), 1)
    lower = jnp.where(col < TILE, mask[1, 0], mask[1, 1])
    return (col <= row) & (jnp.where(row < TILE, mask[0, 0], lower) > 0)


def mix_kernel(mask, rows, mixing, within):
    queries, keys, values = (rows[:, i * 128 : (i + 1) * 128] for i in range(3))
    mixed = jnp.where(allowed_pairs(mask), mt(queries, keys), 0.0).astype(BF16)
    mixing[...] = mixed
    within[...] = mm(mixed, values)


def mix(mask, rows):
    return pl.pallas_call(
        mix_kernel,
        out_shape=(shape(256, 256), shape(256, 128, dtype=F32)),
        in_specs=[SMEM, VMEM],
        out_specs=(VMEM, VMEM),
        **params(2**20, 2 * 256 * 256 * 256),
    )(mask, rows)


def middle_kernel(mask, rows, mixing, within, states, cotangent, attended, early, local_grad):
    queries, keys, values = (rows[:, i * 128 : (i + 1) * 128] for i in range(3))
    carried = jnp.sum(states[...].astype(F32), axis=0).astype(BF16)
    mixture = within[...] + mm(queries, carried)
    inverse_rms = lax.rsqrt(jnp.mean(mixture * mixture, axis=-1, keepdims=True) + epsilon)
    attended[...] = (mixture * inverse_rms).astype(BF16)
    upstream = cotangent[...].astype(F32)
    mixture_grad = (
        inverse_rms * upstream
        - mixture * inverse_rms**3 * jnp.mean(upstream * mixture, axis=-1, keepdims=True)
    ).astype(BF16)
    local_grad[...] = tm(queries, mixture_grad).astype(BF16)
    score_grad = jnp.where(allowed_pairs(mask), mt(mixture_grad, values), 0.0).astype(BF16)
    early[:, :128] = (mm(score_grad, keys) + mt(mixture_grad, carried)).astype(BF16)
    early[:, 128:256] = tm(score_grad, queries).astype(BF16)
    early[:, 256:384] = tm(mixing[...], mixture_grad).astype(BF16)
    early[:, 384:] = rows[:, 128:]


def middle(mask, rows, mixing, within, states, cotangent):
    return pl.pallas_call(
        middle_kernel,
        out_shape=(shape(256, 128), shape(256, 640), shape(128, 128)),
        in_specs=[SMEM] + [VMEM] * 5,
        out_specs=(VMEM,) * 3,
        **params(2**20, 2**28),
    )(mask, rows, mixing, within, states, cotangent)


def finish(early, later, out):
    keys, values = early[:, 384:512], early[:, 512:]
    out[:, :128] = early[:, :128]
    out[:, 128:256] = (early[:, 128:256].astype(F32) + mt(values, later)).astype(BF16)
    out[:, 256:] = (early[:, 256:384].astype(F32) + mm(keys, later)).astype(BF16)


def later_state(states, x):
    return sum(states[y, x].astype(F32) for y in range(4)).astype(BF16)


def parts_kernel(ids, early, states, after, out):
    finish(early, later_state(states, ids[X]), out)


def own_parts(ids, early, states, after):
    return pl.pallas_call(
        parts_kernel,
        out_shape=shape(256, 384),
        in_specs=[SMEM, VMEM, VMEM, ANY],
        out_specs=VMEM,
        **params(2**20, 2**25),
    )(ids, early, states, after)


def back_kernel(ids, early, states, own, other, after, out, *scratch):
    core, x = ids[CORE], ids[X]
    parts, heads, mine, others, sems = scratch
    moves = [pltpu.make_async_copy(early.at[j], heads.at[j], sems.at[j]) for j in range(4)]
    moves.append(pltpu.make_async_copy(own, mine, sems.at[4]))
    moves.append(pltpu.make_async_copy(other, others, sems.at[5]))
    for move in moves:
        move.start()
    for j in range(4):
        moves[j].wait()
        finish(heads.at[j], later_state(states, j), parts.at[j])
    for i, place, weights in ((4, core, mine), (5, 1 - core, others)):
        moves[i].wait()
        total = sum(mt(parts[lax.rem(x + 4 - k, 4)], weights[k]) for k in range(4)).astype(BF16)
        for i in range(4):
            out[:, half(place, i * 256)] = total[:, i * 128 : (i + 1) * 128]


def back_terms(ids, early, states, own, other, after):
    return pl.pallas_call(
        back_kernel,
        out_shape=shape(256, 1024),
        in_specs=[SMEM, ANY, VMEM, ANY, ANY, ANY],
        out_specs=VMEM,
        scratch_shapes=[
            pltpu.VMEM((4, 256, 384), BF16),
            pltpu.VMEM((4, 256, 640), BF16),
            pltpu.VMEM((4, 512, 384), BF16),
            pltpu.VMEM((4, 512, 384), BF16),
            pltpu.SemaphoreType.DMA((6,)),
        ],
        **params(5 * 2**20, 2 * 256 * 4096 * 384),
    )(ids, early, states, own, other, after)


def grads_kernel(events, crossed, parts, other, out):
    for k in range(4):
        rows = slice(k * 512, (k + 1) * 512)
        term = mm(events[rows, :], parts[...]) + mm(crossed[rows, :], other[...])
        out[rows, :] = term.astype(BF16)


def weight_terms(events, crossed, parts, other):
    width = parts.shape[1]
    return pl.pallas_call(
        grads_kernel,
        out_shape=shape(2048, width),
        in_specs=[VMEM] * 4,
        out_specs=VMEM,
        **params(5 * 2**20, 2 * 256 * 4096 * width),
    )(events, crossed, parts, other)


def regroup_kernel(ids, grads, *pieces):
    for k in range(4):
        rows = pl.ds(pl.multiple_of(lax.rem(ids[ZH] + k, 4) * 128, 128), 128)
        pieces[k][...] = grads[rows, :]


def regroup(ids, grads):
    return pl.pallas_call(
        regroup_kernel,
        out_shape=[shape(128, 384)] * 4,
        in_specs=[SMEM, VMEM],
        out_specs=[VMEM] * 4,
        **params(2 * 2**20),
    )(ids, grads)


def sum_kernel(pieces, *refs):
    out = refs[-1]
    summed = sum(pieces[k].astype(F32) for k in range(4)).astype(BF16)
    for k in range(4):
        out[k] = summed


def summed_for_all(pieces, *after):
    return pl.pallas_call(
        sum_kernel,
        out_shape=shape(*pieces.shape),
        in_specs=[VMEM] + [ANY] * len(after),
        out_specs=VMEM,
        **params(2**20),
    )(pieces, *after)


def lay_kernel(pieces, out):
    out[...] = pieces[0]


def lay_out(pieces):
    return pl.pallas_call(
        lay_kernel,
        out_shape=shape(256, 4096),
        grid=(4,),
        in_specs=[pl.BlockSpec((1, 256, 1024), lambda g: (g, 0, 0))],
        out_specs=pl.BlockSpec((256, 1024), lambda g: (0, g)),
        **params(4 * 2**20),
    )(pieces)


def on_device(events, tile_mask, initial_state, w_query, w_key, w_value, cotangent):
    ids = jnp.stack([lax.axis_index(axis) for axis in ("core", "x", "y", "zh")]).astype(jnp.int32)
    shard = jnp.concatenate((w_query, w_key, w_value), axis=1)
    own = spread(lax.all_gather(shard, "zh"), "y").reshape(2048, 384)
    own_events, other_events, own_turned, other_turned = columns(ids, events)
    rows, local_state = project(own_events, other_events, own, swap(own))

    near = lax.all_gather(local_state, ("zh", "core"))
    states = trade(prefix_terms(ids, near, initial_state), "y")
    mixing, within = mix(tile_mask, rows)
    quarters = own.reshape(4, 512, 384)
    back = turn(pick(ids, quarters, near, range(4)), "x")

    attended, early, local_grad = middle(tile_mask, rows, mixing, within, states, cotangent)
    heads = lax.all_gather(early, "x")
    near = lax.all_gather(local_grad, ("zh", "core"))
    sent = prefix_terms(ids, near).reshape(16, 128, 128)
    back_own = join(back, sent)
    back_other = swap(back_own)
    crossed = swap(other_turned)
    states = trade(sent, ("y", "x")).reshape(4, 4, 128, 128)
    parts = own_parts(ids, early, states, crossed)

    grads = weight_terms(own_turned, crossed, parts, swap(parts))
    term = back_terms(ids, heads, states, back_own, back_other, parts)
    summed = summed_for_all(trade(term.reshape(4, 64, 1024), "zl"))
    gathered = trade(summed, "zl").reshape(256, 1024)
    events_grad = lay_out(spread(gathered, "x"))
    grads = lax.psum_scatter(grads, "y", scatter_dimension=0, tiled=True)
    pieces = regroup(ids, grads)
    pieces = [pieces[0]] + [shift(pieces[k], "zh", k) for k in (2, 1, 3)]
    grads = sum(piece.astype(F32) for piece in pieces).astype(BF16)
    return (attended, events_grad, grads[:, :128], grads[:, 128:256], grads[:, 256:])


def solution(mesh):
    fine = Mesh(mesh.devices.reshape(4, 4, 2, 4, 4), CTX + FSDP)
    both = P(CTX, FSDP)
    return jax.shard_map(
        on_device,
        mesh=fine,
        in_specs=(P(CTX, None), P(CTX, None), P(FSDP, None, None), both, both, both, both),
        out_specs=(both, P(CTX, None), both, both, both),
        check_vma=False,
    )
```
